256 devices in a mesh: pipe: 16 (over z, core), dp: 16 (over y, x).
Axes of the slice: x: 4, y: 4, z: 8, core: 2. Of those that a mesh axis runs over, the one named last changes fastest.
Arguments:
- saved: bfloat16 [16, 1, 768, 16384], P('pipe', None, None, 'dp'), may hold values from -6 to 6
- grads_in: bfloat16 [16, 768, 16384], P('pipe', None, 'dp'), may hold values from -6 to 6
- gains: bfloat16 [16, 1, 16384], P('pipe', None, 'dp'), may hold values from 0.25 to 1.75
- w_in: bfloat16 [16, 1, 16384, 1024], P('pipe', None, 'dp'), may hold values from -0.1875 to 0.1875
- w_out_t: bfloat16 [16, 1, 16384, 1024], P('pipe', None, 'dp'), may hold values from -0.046875 to 0.046875
- encoder: bfloat16 [16384, 4096], P('dp', 'pipe'), may hold values from -0.046875 to 0.046875
- enc_bias: float32 [4096], P('pipe'), may hold values from -4 to 4
- decoder: bfloat16 [4096, 16384], P('pipe', 'dp'), may hold values from -0.09375 to 0.09375
- transcoder_norm_gain: bfloat16 [16384], P('dp'), may hold values from 0.25 to 1.75
Outputs:
- grads_out: bfloat16 [16, 768, 16384], P('pipe', None, 'dp')
- grad_encoder: float32 [16384, 4096], P('dp', 'pipe')
- grad_decoder: float32 [4096, 16384], P('pipe', 'dp')
- grad_bias: float32 [4096], P('pipe')
The draws below stay inside these ranges and needn't reach their ends.
All inputs are finite; a program needn't handle non-finite values.
Results may differ from the reference program's by a relative error of at most 0.007.
Values may be sent and summed in bfloat16 or wider, within the bound.
A program may use at most 64 MiB of HBM per device.

```python
import jax
import jax.numpy as jnp
from jax import lax

MODEL_WIDTH = 16384
HID = 1024
WINDOW = 1
TOKENS = 768
SECTIONS = 16
LAT = 4096


def block_levels(rng, shape, cuts, low, high):
    def one(dim, blocks):
        heights = jax.random.uniform(jax.random.fold_in(jax.random.fold_in(rng, 6), dim), (blocks,), jnp.float32, low / len(cuts), high / len(cuts))
        return jnp.repeat(jnp.exp(heights), shape[dim] // blocks).reshape((-1,) + (1,) * (len(shape) - dim - 1))

    level = one(*cuts[0])
    for cut in cuts[1:]:
        level = level * one(*cut)
    return level


def noise(stream_key, extent, spread, bound, cuts=(), kind=jnp.bfloat16):
    entries = spread * jax.random.normal(stream_key, extent, jnp.float32)
    if cuts:
        entries = entries * block_levels(stream_key, extent, cuts, -0.22, 0.18)
    return jnp.clip(entries, -bound, bound).astype(kind)


def setup_inputs(seed: int = 0) -> dict:
    keys = jax.random.split(jax.random.key(seed), 10)
    return {
        "saved": noise(keys[0], (SECTIONS, WINDOW, TOKENS, MODEL_WIDTH), 1.0, 6.0, ((0, 16), (3, 16))),
        "grads_in": noise(keys[1], (SECTIONS, TOKENS, MODEL_WIDTH), 1.0, 6.0, ((0, 16), (2, 16))),
        "gains": jnp.clip(1.0 + 0.15 * jax.random.normal(keys[2], (SECTIONS, WINDOW, MODEL_WIDTH), jnp.float32), 0.25, 1.75).astype(jnp.bfloat16),
        "w_in": noise(keys[3], (SECTIONS, WINDOW, MODEL_WIDTH, HID), HID ** -0.5, 0.1875, ((0, 16), (2, 16))),
        "w_out_t": noise(keys[4], (SECTIONS, WINDOW, MODEL_WIDTH, HID), MODEL_WIDTH ** -0.5, 0.046875, ((0, 16), (2, 16))),
        "encoder": noise(keys[5], (MODEL_WIDTH, LAT), MODEL_WIDTH ** -0.5, 0.046875, ((0, 16), (1, 16))),
        "enc_bias": noise(keys[6], (LAT,), 0.7, 4.0, ((0, 16),), jnp.float32),
        "decoder": noise(keys[7], (LAT, MODEL_WIDTH), LAT ** -0.5, 0.09375, ((0, 16), (1, 16))),
        "transcoder_norm_gain": jnp.clip(1.0 + 0.15 * jax.random.normal(keys[8], (MODEL_WIDTH,), jnp.float32), 0.25, 1.75).astype(jnp.bfloat16),
    }


def norm_statistics(residual_input):
    residual_float = residual_input.astype(jnp.float32)
    inverse_scale = lax.rsqrt(lax.optimization_barrier(jnp.mean(residual_float * residual_float, axis=-1, keepdims=True)) + 1e-05)
    return (inverse_scale, residual_float * inverse_scale)

def layer_back(residual_input, output_gradient, gain, w_in, w_out_t):
    inverse_scale, normalized_input = norm_statistics(residual_input)
    dh = jnp.dot(output_gradient, w_out_t, preferred_element_type=jnp.float32).astype(jnp.bfloat16)
    dnorm = jnp.dot(dh, w_in.T, preferred_element_type=jnp.float32)
    upper_gradient = dnorm * gain.astype(jnp.float32)
    inner_product = lax.optimization_barrier(jnp.mean(upper_gradient * normalized_input, axis=-1, keepdims=True))
    residual_gradient = output_gradient.astype(jnp.float32) + inverse_scale * (upper_gradient - normalized_input * inner_product)
    return residual_gradient.astype(jnp.bfloat16)

def gelu_tanh(v):
    return jax.nn.gelu(v, approximate=True)

def reference(saved, grads_in, gains, w_in, w_out_t, encoder, enc_bias, decoder, transcoder_norm_gain):
    output_gradient = grads_in
    for step in range(WINDOW):

        def one_section(items):
            return layer_back(items[0], items[1], items[2], items[3], items[4])
        residual_gradient = lax.map(one_section, (saved[:, step], output_gradient, gains[:, step], w_in[:, step], w_out_t[:, step]))
        output_gradient = jnp.roll(residual_gradient, -1, 0)
    input_rows = saved[0, 0]
    upstream = output_gradient[0]
    inverse_scale, normalized_input = norm_statistics(input_rows)
    transcoder_norm = (normalized_input * transcoder_norm_gain.astype(jnp.float32)).astype(jnp.bfloat16)
    tpre = jnp.dot(transcoder_norm, encoder, preferred_element_type=jnp.float32) + enc_bias
    latent = gelu_tanh(tpre).astype(jnp.bfloat16)
    dlat = jnp.dot(upstream, decoder.T, preferred_element_type=jnp.float32)
    _, gelu_back = jax.vjp(gelu_tanh, tpre)
    dtpre = gelu_back(dlat)[0].astype(jnp.bfloat16)
    grad_encoder = jnp.dot(transcoder_norm.T, dtpre, preferred_element_type=jnp.float32)
    grad_decoder = jnp.dot(latent.T, upstream, preferred_element_type=jnp.float32)
    grad_bias = lax.optimization_barrier(jnp.sum(dtpre.astype(jnp.float32), axis=0))
    return (output_gradient, grad_encoder, grad_decoder, grad_bias)
```

```python
import functools

import jax
import jax.numpy as jnp
from jax import lax
from jax.experimental import pallas as pl
from jax.experimental.pallas import tpu as pltpu
from jax.sharding import PartitionSpec as P

MESH = pl.DeviceIdType.MESH
BF = jnp.bfloat16
F32 = jnp.float32
MODEL_WIDTH = 16384
T, W, H, L = 768, 1024, 1024, 256
C, TC = 3, 256
Q, QW = 4, 256
DP, PIPE = 16, 16
TS = TC // DP
BLK = 64
HALF = T // 2
NB = HALF // BLK
TN_FIRST = 2
GELU_A = 0.7978845608028654
GELU_B = 0.044715


def dot(a, b, dims=((1,), (0,))):
    return lax.dot_general(a, b, (dims, ((), ())), preferred_element_type=F32)


def row_total(block):
    lanes = block[:, 0:128]
    for j in range(1, block.shape[1] // 128):
        lanes = lanes + block[:, j * 128 : (j + 1) * 128]
    return jnp.sum(lanes.T, axis=0, keepdims=True)


def as_columns(row):
    return jnp.broadcast_to(row, (128, row.shape[1])).T


def kernel(
    gains, bias, tgain, saved, gin, win, wout, enc, dec,
    gout, genc, gdec, gbias,
    x_v, gin_v, win_v, wout_v, enc_v, dec_v,
    dhp, r0, r1, r2, r3, s1, k1, s2, k2, s3, k3, dhf, uf, dx, tn, gt,
    sqb, ipb, rcol, part, rsb, tps, full, ge_v, gd_v,
    load_sem, rs_send, rs_recv, sq_sem, ip_send, ip_recv, tr_send, tr_recv,
    tn_recv, tn_send, tnx_recv, gt_recv, gt_send, gtx_recv, go_send, go_recv, out_sem,
):
    p = lax.axis_index("pipe")
    d = lax.axis_index("dp")
    z, core = p // 2, p % 2
    y, x = d // 4, d % 4
    bits = (((x + 1) // 2) % 2, x // 2, ((y + 1) // 2) % 2, y // 2)
    peers = (
        y * 4 + (x + 1 - 2 * (x % 2)),
        y * 4 + (3 - x),
        (y + 1 - 2 * (y % 2)) * 4 + x,
        (3 - y) * 4 + x,
    )
    partner = p + 1 - 2 * core
    up, down = (p + 2) % PIPE, (p + PIPE - 2) % PIPE

    def local(src, dst, sem):
        return pltpu.make_async_copy(src, dst, sem)

    def send(src, dst, ssem, rsem, to_p, to_d):
        pltpu.make_async_remote_copy(
            src_ref=src, dst_ref=dst, send_sem=ssem, recv_sem=rsem,
            device_id=(to_p, to_d), device_id_type=MESH,
        ).start()

    def await_bytes(ref, sem):
        pltpu.make_async_copy(ref, ref, sem).wait()

    def rows(c, n=TC):
        return pl.ds(c * n, n)

    gin_l = [local(gin.at[0, rows(c)], gin_v.at[rows(c)], load_sem.at[c]) for c in range(C)]
    wout_l = local(wout.at[0, 0], wout_v, load_sem.at[3])
    x_l = local(saved.at[0, 0], x_v, load_sem.at[4])
    win_l = local(win.at[0, 0], win_v, load_sem.at[5])
    enc_l = local(enc, enc_v, load_sem.at[6])
    dec_l = local(dec, dec_v, load_sem.at[7])
    for copy in (wout_l, *gin_l, x_l, win_l, enc_l, dec_l):
        copy.start()

    barrier = pltpu.get_barrier_semaphore()

    def greet(k, _):
        pl.semaphore_signal(barrier, inc=1, device_id=(p, (d + k) % DP), device_id_type=MESH)
        return 0

    lax.fori_loop(1, DP, greet, 0)
    for by in (1, 2, PIPE - 2, PIPE - 1):
        pl.semaphore_signal(barrier, inc=1, device_id=((p + by) % PIPE, d), device_id_type=MESH)

    offs = []
    for q in range(Q):
        o = [0]
        for s in range(4):
            o.append(o[-1] + bits[(q + s) % 4] * (128 >> s))
        offs.append(o)

    def at(c, off, n):
        return pl.ds(pl.multiple_of(c * TC + off, n), n)

    def dh_partial(c):
        for q in range(Q):
            dhp[q, rows(c)] = dot(gin_v[rows(c)], wout_v[:, q * QW : (q + 1) * QW]).astype(BF)

    def dh_send(c):
        for q in range(Q):
            b = q % 4
            send(dhp.at[q, at(c, (1 - bits[b]) * 128, 128)], r0.at[c, q],
                 rs_send.at[c, 0], rs_recv.at[c, 0], p, peers[b])

    def step_bytes(c, s):
        if s < 4:
            return (r0, r1, r2, r3)[s].at[c]
        return r0.at[c, :, pl.ds(0, TS << (s - 4))]

    def cols(q):
        return slice(q * QW, (q + 1) * QW)

    def exchange_step(c, s):
        await_bytes(step_bytes(c, s), rs_recv.at[c, s])
        if s == 7:
            return
        for q in range(Q):
            if s < 3:
                n = 64 >> s
                v = bits[(q + s + 1) % 4]
                peer = peers[(q + s + 1) % 4]
                give, keep = (pl.ds(pl.multiple_of(w * n, n), n) for w in (1 - v, v))
                if s == 0:
                    mine = offs[q][1]
                    dst = r1
                    s1[c, q] = (dhp[q, at(c, mine + (1 - v) * n, n)].astype(F32)
                                + r0[c, q, give].astype(F32)).astype(BF)
                    send(s1.at[c, q], r1.at[c, q], rs_send.at[c, 1], rs_recv.at[c, 1], p, peer)
                    k1[c, q] = dhp[q, at(c, mine + v * n, n)].astype(F32) + r0[c, q, keep].astype(F32)
                elif s == 1:
                    s2[c, q] = k1[c, q, give] + r1[c, q, give].astype(F32)
                    send(s2.at[c, q], r2.at[c, q], rs_send.at[c, 2], rs_recv.at[c, 2], p, peer)
                    k2[c, q] = k1[c, q, keep] + r1[c, q, keep].astype(F32)
                else:
                    s3[c, q] = k2[c, q, give] + r2[c, q, give]
                    send(s3.at[c, q], r3.at[c, q], rs_send.at[c, 3], rs_recv.at[c, 3], p, peer)
                    k3[c, q] = k2[c, q, keep] + r2[c, q, keep]
            else:
                b = (q + 6 - s) % 4
                n = TS << (s - 3)
                own = at(c, offs[q][7 - s], n)
                if s == 3:
                    dhf[own, cols(q)] = (k3[c, q] + r3[c, q]).astype(BF)
                send(dhf.at[own, cols(q)], dhf.at[own, cols(q)],
                     rs_send.at[c, s + 1], rs_recv.at[c, s + 1], p, peers[b])

    def to_group(src_of, dst_of, ssem, rsem):
        def one(k, _):
            j = (d + k) % DP
            send(src_of(j), dst_of(j), ssem, rsem, p, j)
            return 0

        lax.fori_loop(1, DP, one, 0)

    tn_hop = z + core * (8 - 2 * z)
    tn_next = (p + 2 - 4 * core + PIPE) % PIPE

    def tn_forward(k):
        blk = pl.ds(pl.multiple_of(core * HALF + k * BLK, BLK), BLK)
        await_bytes(tn.at[blk], tn_recv.at[k])

        @pl.when(tn_hop < 7)
        def _():
            send(tn.at[blk], tn.at[blk], tn_send.at[0], tn_recv.at[k], tn_next, d)

        send(tn.at[blk], tn.at[blk], tn_send.at[2], tnx_recv, partner, d)

    def tn_gap(g):
        k = g - TN_FIRST - 2 * (tn_hop - 1)

        @pl.when((z > 0) & (k >= 0) & (k < NB))
        def _():
            tn_forward(k)

    def tn_rest(g):
        def one(k, _):
            tn_forward(k)
            return 0

        @pl.when(z > 0)
        def _():
            lax.fori_loop(jnp.clip(g - TN_FIRST - 2 * (tn_hop - 1), 0, NB), NB, one, 0)
            await_bytes(tn.at[pl.ds(0, HALF)], tnx_recv)

        @pl.when(p == 1)
        def _():
            await_bytes(tn, tnx_recv)

    def gt_forward(k):
        blk = pl.ds(pl.multiple_of(k * BLK, BLK), BLK)
        await_bytes(gt.at[blk], gt_recv.at[k])

        @pl.when(z < 7)
        def _():
            send(gt.at[blk], gt.at[blk], gt_send.at[0], gt_recv.at[k], up, d)

        send(gt.at[blk], gt.at[blk], gt_send.at[1], gtx_recv.at[k // (TC // BLK)], partner, d)

    wout_l.wait()
    gin_l[0].wait()
    dh_partial(0)
    pl.semaphore_wait(barrier, DP - 1 + 4)
    dh_send(0)
    x_l.wait()
    for c in range(C):
        xf = x_v[rows(c)].astype(F32)
        sqb[d, :, c * TC : (c + 1) * TC] = row_total(xf * xf)
    to_group(lambda j: sqb.at[d], lambda j: sqb.at[d], sq_sem.at[0], sq_sem.at[1])
    for c in range(1, C):
        gin_l[c].wait()
        dh_partial(c)
        dh_send(c)
    await_bytes(sqb.at[pl.ds(0, DP - 1)], sq_sem.at[1])
    squares = jnp.sum(sqb[...], axis=0)
    scale = lax.rsqrt(squares / MODEL_WIDTH + 1e-05)
    for c in range(C):
        rcol[rows(c)] = as_columns(scale[:, c * TC : (c + 1) * TC])

    @pl.when(p == 0)
    def _():
        def one(b, _):
            blk = pl.ds(pl.multiple_of(b * BLK, BLK), BLK)
            r = rcol[blk]
            for j in range(W // 128):
                js = slice(j * 128, (j + 1) * 128)
                tn[blk, js] = (x_v[blk, js].astype(F32) * r * tgain[:, js].astype(F32)).astype(BF)
            return 0

        def both(b, _):
            for stream in (0, 1):
                k = b + stream * NB
                one(k, 0)
                blk = pl.ds(pl.multiple_of(k * BLK, BLK), BLK)
                send(tn.at[blk], tn.at[blk], tn_send.at[stream], tn_recv.at[b],
                     up if stream == 0 else PIPE - 1, d)
            return 0

        lax.fori_loop(0, NB, both, 0)
        send(tn, tn, tn_send.at[2], tnx_recv, partner, d)

    win_l.wait()

    def back(c):
        lanes = jnp.zeros((1, TC), F32)
        for j in range(W // 256):
            js = slice(j * 256, (j + 1) * 256)
            u = dot(dhf[rows(c)], win_v[js, :], ((1,), (1,))) * gains[:, js].astype(F32)
            uf[rows(c), js] = u
            lanes = lanes + row_total(u * x_v[rows(c), js].astype(F32))
        ipb[c, d] = lanes
        to_group(lambda j: ipb.at[c, d], lambda j: ipb.at[c, d], ip_send.at[c], ip_recv.at[c])

    def finish(c):
        await_bytes(ipb.at[c, pl.ds(0, DP - 1)], ip_recv.at[c])
        inner = as_columns(jnp.sum(ipb[c], axis=0))
        r = rcol[rows(c)]
        coef = r * r * r * inner * (1.0 / MODEL_WIDTH)
        for j in range(W // 128):
            js = slice(j * 128, (j + 1) * 128)
            v = (gin_v[rows(c), js].astype(F32) + r * uf[rows(c), js]
                 - x_v[rows(c), js].astype(F32) * coef).astype(BF)
            dx[rows(c), js] = v

        @pl.when(p == 1)
        def _():
            gt[rows(c)] = dx[rows(c)]

            def one(i, _):
                k = c * (TC // BLK) + i
                blk = pl.ds(pl.multiple_of(k * BLK, BLK), BLK)
                send(dx.at[blk], gt.at[blk], gt_send.at[0], gt_recv.at[k], up, d)
                return 0

            lax.fori_loop(0, TC // BLK, one, 0)
            send(dx.at[rows(c)], gt.at[rows(c)], gt_send.at[1], gtx_recv.at[c], partner, d)

        send(dx.at[rows(c)], gout.at[0, rows(c)], go_send.at[c], go_recv.at[c],
             (p + PIPE - 1) % PIPE, d)

    g = 0
    for tau in range(8 + 2 * (C - 1) + 1):
        for c in range(C):
            s = tau - 2 * c
            if s == 8:
                finish(c)
            elif 0 <= s < 8:
                exchange_step(c, s)
                if s == 7:
                    back(c)
            else:
                continue
            tn_gap(g)
            g += 1
    tn_rest(g)

    def shard(c):
        return pl.ds(pl.multiple_of(c * TC + d * TS, TS), TS)

    def scatter(kind, c, a, b, dims):
        part[kind, rows(c)] = dot(a, b, dims).astype(BF)
        to_group(
            lambda j: part.at[kind, pl.ds(pl.multiple_of(c * TC + j * TS, TS), TS)],
            lambda j: rsb.at[kind, c, d], tr_send.at[2 * kind, c], tr_recv.at[2 * kind, c])
        rsb[kind, c, d] = part[kind, shard(c)]

    def total(kind, c):
        await_bytes(rsb.at[kind, c, pl.ds(0, DP - 1)], tr_recv.at[2 * kind, c])
        return jnp.sum(rsb[kind, c].astype(F32), axis=0)

    def gather(kind, c, values):
        full[kind, shard(c)] = values.astype(BF)
        to_group(
            lambda j: full.at[kind, shard(c)], lambda j: full.at[kind, shard(c)],
            tr_send.at[2 * kind + 1, c], tr_recv.at[2 * kind + 1, c])

    def gathered(kind, c):
        await_bytes(rsb.at[kind, c, pl.ds(0, DP - 1)], tr_recv.at[2 * kind + 1, c])

    enc_l.wait()
    for c in range(C):
        scatter(0, c, tn[rows(c)], enc_v[...], ((1,), (0,)))
    for c in range(C):
        v = total(0, c) + bias[...]
        tps[c] = v
        gather(0, c, 0.5 * v * (1.0 + jnp.tanh(GELU_A * (v + GELU_B * v * v * v))))
    dec_l.wait()
    for c in range(C):
        @pl.when((core == 1) & (z > 0))
        def _():
            def one(k, _):
                gt_forward(k)
                return 0

            lax.fori_loop(c * (TC // BLK), (c + 1) * (TC // BLK), one, 0)

        @pl.when(core == 0)
        def _():
            await_bytes(gt.at[rows(c)], gtx_recv.at[c])

        scatter(1, c, gt[rows(c)], dec_v[...], ((1,), (1,)))
    for c in range(C):
        v = tps[c]
        th = jnp.tanh(GELU_A * (v + GELU_B * v * v * v))
        slope = 0.5 * (1.0 + th) + 0.5 * v * (1.0 - th * th) * GELU_A * (1.0 + 3.0 * GELU_B * v * v)
        gather(1, c, total(1, c) * slope)
    for c in range(C):
        gathered(0, c)
    for j in range(W // 256):
        js = slice(j * 256, (j + 1) * 256)
        gd_v[:, js] = dot(full[0], gt[:, js], ((0,), (0,)))
    gd_out = local(gd_v, gdec, out_sem.at[0])
    gd_out.start()
    for c in range(C):
        gathered(1, c)
    for j in range(W // 256):
        js = slice(j * 256, (j + 1) * 256)
        ge_v[js, :] = dot(tn[:, js], full[1], ((0,), (0,)))
    ge_out = local(ge_v, genc, out_sem.at[1])
    ge_out.start()
    gbias[...] = jnp.sum(full[1].astype(F32), axis=0, keepdims=True)

    for c in range(C):
        await_bytes(dx.at[rows(c)], go_recv.at[c])
        await_bytes(dx.at[rows(c)], go_send.at[c])
        for s in range(8):
            await_bytes(step_bytes(c, s), rs_send.at[c, s])
        await_bytes(ipb.at[c, pl.ds(0, DP - 1)], ip_send.at[c])
        for kind in range(4):
            await_bytes(rsb.at[0, c, pl.ds(0, DP - 1)], tr_send.at[kind, c])
    await_bytes(sqb.at[pl.ds(0, DP - 1)], sq_sem.at[0])

    @pl.when(p == 0)
    def _():
        await_bytes(tn.at[pl.ds(0, HALF)], tn_send.at[0])
        await_bytes(tn.at[pl.ds(0, HALF)], tn_send.at[1])
        await_bytes(tn, tn_send.at[2])

    @pl.when(z > 0)
    def _():
        @pl.when(tn_hop < 7)
        def _():
            await_bytes(tn.at[pl.ds(0, HALF)], tn_send.at[0])

        await_bytes(tn.at[pl.ds(0, HALF)], tn_send.at[2])

    @pl.when(core == 1)
    def _():
        @pl.when(z < 7)
        def _():
            await_bytes(gt, gt_send.at[0])

        await_bytes(gt, gt_send.at[1])

    gd_out.wait()
    ge_out.wait()


def body(saved, grads_in, gains, w_in, w_out_t, encoder, enc_bias, decoder, transcoder_norm_gain):
    vmem = pl.BlockSpec(memory_space=pltpu.VMEM)
    anywhere = pl.BlockSpec(memory_space=pl.ANY)
    V = pltpu.VMEM
    DMA = pltpu.SemaphoreType.DMA
    scratch = [
        V((T, W), BF), V((T, W), BF), V((W, H), BF), V((W, H), BF), V((W, L), BF), V((L, W), BF),
        V((Q, T, QW), BF),
        V((C, Q, 128, QW), BF), V((C, Q, 64, QW), BF), V((C, Q, 32, QW), F32), V((C, Q, 16, QW), F32),
        V((C, Q, 64, QW), BF), V((C, Q, 64, QW), F32),
        V((C, Q, 32, QW), F32), V((C, Q, 32, QW), F32),
        V((C, Q, 16, QW), F32), V((C, Q, 16, QW), F32),
        V((T, H), BF), V((T, W), F32), V((T, W), BF), V((T, W), BF), V((T, W), BF),
        V((DP, 1, T), F32), V((C, DP, 1, TC), F32), V((T, 128), F32),
        V((2, T, L), BF), V((2, C, DP, TS, L), BF), V((C, TS, L), F32), V((2, T, L), BF),
        V((W, L), F32), V((L, W), F32),
        DMA((8,)), DMA((C, 8)), DMA((C, 8)), DMA((2,)), DMA((C,)), DMA((C,)), DMA((4, C)), DMA((4, C)),
        DMA((NB,)), DMA((3,)), DMA, DMA((2 * NB,)), DMA((2,)), DMA((C,)), DMA((C,)), DMA((C,)), DMA((2,)),
    ]
    gout, genc, gdec, gbias = pl.pallas_call(
        kernel,
        out_shape=(
            jax.ShapeDtypeStruct((1, T, W), BF),
            jax.ShapeDtypeStruct((W, L), F32),
            jax.ShapeDtypeStruct((L, W), F32),
            jax.ShapeDtypeStruct((1, L), F32),
        ),
        in_specs=[vmem] * 3 + [anywhere] * 6,
        out_specs=(anywhere, anywhere, anywhere, vmem),
        scratch_shapes=scratch,
        compiler_params=pltpu.CompilerParams(
            collective_id=0, has_side_effects=True, vmem_limit_bytes=56 * 1024 * 1024
        ),
        cost_estimate=pl.CostEstimate(flops=5_000_000_000, bytes_accessed=14_000_000, transcendentals=0),
    )(
        gains[0], enc_bias[None], transcoder_norm_gain[None],
        saved, grads_in, w_in, w_out_t, encoder, decoder,
    )
    return gout, genc, gdec, gbias[0]


def solution(mesh):
    in_specs = (
        P("pipe", None, None, "dp"),
        P("pipe", None, "dp"),
        P("pipe", None, "dp"),
        P("pipe", None, "dp", None),
        P("pipe", None, "dp", None),
        P("dp", "pipe"),
        P("pipe"),
        P("pipe", "dp"),
        P("dp"),
    )
    out_specs = (P("pipe", None, "dp"), P("dp", "pipe"), P("pipe", "dp"), P("pipe"))
    return jax.shard_map(body, mesh=mesh, in_specs=in_specs, out_specs=out_specs, check_vma=False)
```

```python
import functools

import jax
import jax.numpy as jnp
from jax import lax
from jax.experimental import pallas as pl
from jax.experimental.pallas import tpu as pltpu
from jax.sharding import PartitionSpec as P

MESH = pl.DeviceIdType.MESH
BF = jnp.bfloat16
F32 = jnp.float32
MODEL_WIDTH = 16384
T, W, H, L = 768, 1024, 1024, 256
C, TC = 3, 256
HW = H // 2
XR, YR = TC // 4, TC // 16
DP, PIPE = 16, 16
TS = TC // DP
BLK = 32
HALF = T // 2
NB = HALF // BLK
GB = 32
GN = TC // GB
X0_AT = {"00": 8, "10": 10, "01": 14, "20": 16, "11": 18, "02": 20, "21": 22, "12": 24, "22": 64}
GT_LAG = 3
GT_AT = {"13": 3, "0f": 5, "23": 8, "1f": 11, "2f": 14}
GO_AFTER = "00"
Z_UP = 4
GELU_A = 0.7978845608028654
GELU_B = 0.044715


def dot(a, b, dims=((1,), (0,))):
    return lax.dot_general(a, b, (dims, ((), ())), preferred_element_type=F32)


def row_total(block):
    lanes = block[:, 0:128]
    for j in range(1, block.shape[1] // 128):
        lanes = lanes + block[:, j * 128 : (j + 1) * 128]
    return jnp.sum(lanes.T, axis=0, keepdims=True)


def as_columns(row):
    return jnp.broadcast_to(row, (128, row.shape[1])).T


def kernel(
    gains, bias, tgain, saved, gin, win, wout, enc, dec,
    gout, genc, gdec, gbias,
    x_v, gin_v, win_v, wout_v, enc_v, dec_v,
    dhp, p1r, p2s, p2r, dhf, uf, dx, x0, tn, gt, r0,
    sqb, ipb, rcol, part, rsb, tps, full, ge_v, gd_v,
    load_sem, rs_send, rs_recv, sq_sem, ip_send, ip_recv, tr_send, tr_recv,
    tn_recv, tn_send, tnx_recv, gt_recv, gt_send, gtx_recv, go_send, go_recv, out_sem, r0_sem, turn,
):
    p = lax.axis_index("pipe")
    d = lax.axis_index("dp")
    z, core = p // 2, p % 2
    y, x = d // 4, d % 4
    partner = p + 1 - 2 * core
    up, down = (p + 2) % PIPE, (p + PIPE - 2) % PIPE
    first = core == jnp.where(z == 0, 1, 0)
    carries_x0, carries_gt = (core == 1) & (z > 0), (core == 0) & (z > 0)

    def local(src, dst, sem):
        return pltpu.make_async_copy(src, dst, sem)

    def send(src, dst, ssem, rsem, to_p, to_d):
        pltpu.make_async_remote_copy(
            src_ref=src, dst_ref=dst, send_sem=ssem, recv_sem=rsem,
            device_id=(to_p, to_d), device_id_type=MESH,
        ).start()

    def await_bytes(ref, sem):
        pltpu.make_async_copy(ref, ref, sem).wait()

    def rows(c, n=TC):
        return pl.ds(c * n, n)

    gin_l = [local(gin.at[0, rows(c)], gin_v.at[rows(c)], load_sem.at[c]) for c in range(C)]
    wout_l = local(wout.at[0, 0], wout_v, load_sem.at[3])
    x_l = local(saved.at[0, 0], x_v, load_sem.at[4])
    win_l = local(win.at[0, 0], win_v, load_sem.at[5])
    enc_l = local(enc, enc_v, load_sem.at[6])
    dec_l = local(dec, dec_v, load_sem.at[7])
    for copy in (wout_l, *gin_l, x_l, win_l, enc_l, dec_l):
        copy.start()

    barrier = pltpu.get_barrier_semaphore()

    def greet(k, _):
        pl.semaphore_signal(barrier, inc=1, device_id=(p, (d + k) % DP), device_id_type=MESH)
        return 0

    lax.fori_loop(1, DP, greet, 0)
    for by in (1, 2, PIPE - 2, PIPE - 1):
        pl.semaphore_signal(barrier, inc=1, device_id=((p + by) % PIPE, d), device_id_type=MESH)

    @pl.when((p > 2) & (p < PIPE - 2))
    def _():
        pl.semaphore_signal(barrier, inc=1, device_id=(0, d), device_id_type=MESH)

    @pl.when(p == PIPE - 2)
    def _():
        pl.semaphore_signal(barrier, inc=1, device_id=(1, d), device_id_type=MESH)


    place = ((x, y), (y, x))

    def peer(h, axis, k):
        to = (place[h][axis] + k) % 4
        return (y * 4 + to if h == axis else to * 4 + x), to

    def some(start, n):
        return pl.ds(pl.multiple_of(start, n), n)

    def cols(h):
        return slice(h * HW, (h + 1) * HW)

    def dh_partial(c):
        for j in range(H // 256):
            js = slice((j % 2) * 256, (j % 2 + 1) * 256)
            dhp[j // 2, rows(c), js] = dot(gin_v[rows(c)], wout_v[:, j * 256 : (j + 1) * 256]).astype(BF)

    def dh_send():
        def one(c, _):
            for k in (1, 2, 3):
                for h in (0, 1):
                    j, to = peer(h, 0, k)
                    send(dhp.at[h, some(c * TC + to * XR, XR)], p1r.at[c, h, k - 1],
                         rs_send.at[c, 0], rs_recv.at[c, 0], p, j)
            return 0

        lax.fori_loop(0, C, one, 0)

    def step_bytes(c, s):
        return (p1r.at[c], p2r.at[c], p1r.at[c, :, :, pl.ds(0, YR)], p1r.at[c])[s]

    def exchange_step(c, s):
        await_bytes(step_bytes(c, s), rs_recv.at[c, s])
        for h in (0, 1):
            i, j = place[h]
            mine = c * TC + i * XR
            if s == 0:
                v = dhp[h, some(mine, XR)].astype(F32)
                for k in range(3):
                    v = v + p1r[c, h, k].astype(F32)
                p2s[c, h] = v
            elif s == 1:
                v = p2s[c, h, some(j * YR, YR)]
                for k in range(3):
                    v = v + p2r[c, h, k]
                dhf[some(mine + j * YR, YR), cols(h)] = v.astype(BF)
            for k in (1, 2, 3):
                if s == 0:
                    to_d, to = peer(h, 1, k)
                    send(p2s.at[c, h, some(to * YR, YR)], p2r.at[c, h, k - 1],
                         rs_send.at[c, 1], rs_recv.at[c, 1], p, to_d)
                elif s < 3:
                    own = some(mine + j * YR, YR) if s == 1 else some(mine, XR)
                    to_d, _ = peer(h, 1 if s == 1 else 0, k)
                    send(dhf.at[own, cols(h)], dhf.at[own, cols(h)],
                         rs_send.at[c, s + 1], rs_recv.at[c, s + 1], p, to_d)

    def to_group(src_of, dst_of, ssem, rsem):
        def one(k, _):
            j = (d + k) % DP
            send(src_of(j), dst_of(j), ssem, rsem, p, j)
            return 0

        lax.fori_loop(1, DP, one, 0)

    def x0_forward(stream, k):
        blk = pl.ds(pl.multiple_of(stream * HALF + k * BLK, BLK), BLK)
        sem = tn_recv.at[stream * NB + k]
        await_bytes(x0.at[blk], sem)

        @pl.when(z < 7 if stream == 0 else z > 1)
        def _():
            send(x0.at[blk], x0.at[blk], tn_send.at[stream], sem, (up, down)[stream], d)

        send(x0.at[blk], x0.at[blk], tn_send.at[2], tnx_recv, partner, d)

    def x0_done(stream, m):
        hops = z - 1 if stream == 0 else 7 - z
        return jnp.clip(m - 3 * hops, 0, NB)

    def x0_blocks(lo, hi):
        @pl.when(carries_x0)
        def _():
            for stream in (0, 1):
                def one(k, _, stream=stream):
                    x0_forward(stream, k)
                    return 0

                lax.fori_loop(x0_done(stream, lo), x0_done(stream, hi), one, 0)

    def tnorm():
        @pl.when((p == 1) | carries_gt)
        def _():
            await_bytes(x0, tnx_recv)

        @pl.when(p > 0)
        def _():
            await_bytes(r0, r0_sem.at[1])

        tg = tgain[...].astype(F32)[None, :]
        for c in range(C):
            r = as_columns(r0[:, c * TC : (c + 1) * TC])
            for j in range(W // 128):
                js = slice(j * 128, (j + 1) * 128)
                tn[rows(c), js] = (x0[rows(c), js].astype(F32) * r * tg[:, js]).astype(BF)

    goes_up = z <= Z_UP
    gt_hop = jnp.where(goes_up, z, 8 - z)
    gt_last = (z == Z_UP) | (z == Z_UP + 1)
    gt_next = jnp.where(goes_up, up, down)
    gt_root_down = Z_UP < 7

    def gt_forward(k):
        blk = pl.ds(pl.multiple_of(k * GB, GB), GB)
        await_bytes(gt.at[blk], gt_recv.at[k])

        @pl.when(jnp.logical_not(gt_last))
        def _():
            send(gt.at[blk], gt.at[blk], gt_send.at[0], gt_recv.at[k], gt_next, d)

        send(gt.at[blk], gt.at[blk], gt_send.at[1], gtx_recv.at[k // GN], partner, d)

    def gt_done(m):
        return jnp.clip(m - GT_LAG * (gt_hop - 1), 0, C * GN)

    def gt_blocks(lo, hi):
        def one(k, _):
            gt_forward(k)
            return 0

        @pl.when(carries_gt)
        def _():
            lax.fori_loop(lo, hi, one, 0)

    wout_l.wait()
    for c in range(C):
        gin_l[c].wait()
        dh_partial(c)
    pl.semaphore_wait(barrier, jnp.where(p == 0, DP + PIPE - 2, DP - 1 + 4 + jnp.where(p == 1, 1, 0)))
    pl.when(first)(dh_send)
    x_l.wait()

    @pl.when(p == 0)
    def _():
        x0[...] = x_v[...]

        def one(b, _):
            for stream in (0, 1):
                blk = pl.ds(pl.multiple_of(stream * HALF + b * BLK, BLK), BLK)
                send(x_v.at[blk], x0.at[blk], tn_send.at[stream], tn_recv.at[stream * NB + b],
                     3 if stream == 0 else PIPE - 1, d)
            return 0

        lax.fori_loop(0, NB, one, 0)
        send(x_v, x0, tn_send.at[2], tnx_recv, partner, d)

    for c in range(C):
        xf = x_v[rows(c)].astype(F32)
        sqb[d, :, c * TC : (c + 1) * TC] = row_total(xf * xf)
    to_group(lambda j: sqb.at[d], lambda j: sqb.at[d], sq_sem.at[0], sq_sem.at[1])

    def scale_ready():
        await_bytes(sqb.at[pl.ds(0, DP - 1)], sq_sem.at[1])
        squares = jnp.sum(sqb[...], axis=0)
        scale = lax.rsqrt(squares / MODEL_WIDTH + 1e-05)
        for c in range(C):
            rcol[rows(c)] = as_columns(scale[:, c * TC : (c + 1) * TC])

    @pl.when(p == 0)
    def _():
        scale_ready()
        squares = jnp.sum(sqb[...], axis=0)
        r0[...] = lax.rsqrt(squares / MODEL_WIDTH + 1e-05)

        def one(k, _):
            send(r0, r0, r0_sem.at[0], r0_sem.at[1], k, d)
            return 0

        lax.fori_loop(1, PIPE, one, 0)

    @pl.when(jnp.logical_not(first))
    def _():
        pl.semaphore_wait(turn, 1)
        dh_send()

    win_l.wait()
    enc_l.wait()
    dec_l.wait()

    def back(c):
        lanes = jnp.zeros((1, TC), F32)
        for j in range(W // 256):
            js = slice(j * 256, (j + 1) * 256)
            u = dot(dhf[rows(c)], win_v[js, :], ((1,), (1,))) * gains[:, js].astype(F32)
            uf[rows(c), js] = u
            lanes = lanes + row_total(u * x_v[rows(c), js].astype(F32))
        ipb[c, d] = lanes
        to_group(lambda j: ipb.at[c, d], lambda j: ipb.at[c, d], ip_send.at[c], ip_recv.at[c])

    dx_late = carries_gt & (z > Z_UP + 1)

    def pass_dx(c):
        send(dx.at[rows(c)], gout.at[0, rows(c)], go_send.at[c], go_recv.at[c],
             (p + PIPE - 1) % PIPE, d)

    def finish(c):
        await_bytes(ipb.at[c, pl.ds(0, DP - 1)], ip_recv.at[c])
        inner = as_columns(jnp.sum(ipb[c], axis=0))
        r = rcol[rows(c)]
        coef = r * r * r * inner * (1.0 / MODEL_WIDTH)
        for j in range(W // 128):
            js = slice(j * 128, (j + 1) * 128)
            v = (gin_v[rows(c), js].astype(F32) + r * uf[rows(c), js]
                 - x_v[rows(c), js].astype(F32) * coef).astype(BF)
            dx[rows(c), js] = v

        @pl.when(p == 1)
        def _():
            gt[rows(c)] = dx[rows(c)]

            def one(k, _):
                blk = pl.ds(pl.multiple_of(k * GB, GB), GB)
                send(dx.at[blk], gt.at[blk], gt_send.at[0], gt_recv.at[k], 2, d)
                if gt_root_down:
                    send(dx.at[blk], gt.at[blk], gt_send.at[2], gt_recv.at[k], PIPE - 2, d)
                return 0

            lax.fori_loop(c * GN, (c + 1) * GN, one, 0)
            send(dx.at[rows(c)], gt.at[rows(c)], gt_send.at[1], gtx_recv.at[c], partner, d)

        pl.when(jnp.logical_not(dx_late))(lambda: pass_dx(c))

    def shard(c):
        return pl.ds(pl.multiple_of(c * TC + d * TS, TS), TS)

    def scatter(kind, c, a, b, dims):
        part[kind, rows(c)] = dot(a, b, dims).astype(BF)
        to_group(
            lambda j: part.at[kind, pl.ds(pl.multiple_of(c * TC + j * TS, TS), TS)],
            lambda j: rsb.at[kind, c, d], tr_send.at[2 * kind, c], tr_recv.at[2 * kind, c])
        rsb[kind, c, d] = part[kind, shard(c)]

    def total(kind, c):
        await_bytes(rsb.at[kind, c, pl.ds(0, DP - 1)], tr_recv.at[2 * kind, c])
        return jnp.sum(rsb[kind, c].astype(F32), axis=0)

    def gather(kind, c, values):
        full[kind, shard(c)] = values.astype(BF)
        to_group(
            lambda j: full.at[kind, shard(c)], lambda j: full.at[kind, shard(c)],
            tr_send.at[2 * kind + 1, c], tr_recv.at[2 * kind + 1, c])

    def gathered(kind, c):
        await_bytes(rsb.at[kind, c, pl.ds(0, DP - 1)], tr_recv.at[2 * kind + 1, c])

    def tpre_partial():
        tnorm()
        for c in range(C):
            scatter(0, c, tn[rows(c)], enc_v[...], ((1,), (0,)))

    early_tnorm = carries_x0 | (p == 0)
    order = ("00", "10", "01", "20", "11", "02", "21", "12", "22", "03", "13", "0f", "23", "1f", "2f")
    gt_now = 0
    x0_now = 0
    for step in order:
        c = int(step[0])
        if step in X0_AT:
            x0_blocks(x0_now, X0_AT[step])
            x0_now = X0_AT[step]
        if step[1] == "f":
            finish(c)
        else:
            exchange_step(c, int(step[1]))
            if step[1] == "3":
                back(c)
            if step == GO_AFTER:
                @pl.when(first)
                def _():
                    pl.semaphore_signal(turn, inc=1, device_id=(partner, d), device_id_type=MESH)
        if step == "12":
            pl.when(p > 0)(scale_ready)
        if step == "22":
            pl.when(early_tnorm)(tpre_partial)
        if step in GT_AT:
            gt_blocks(gt_done(gt_now), gt_done(GT_AT[step]))
            gt_now = GT_AT[step]

    def gt_chunk(c):
        if c < C - 1:
            gt_blocks(jnp.clip(gt_done(gt_now), c * GN, (c + 1) * GN), (c + 1) * GN)

        @pl.when(carries_x0 | (p == 0))
        def _():
            await_bytes(gt.at[rows(c)], gtx_recv.at[c])

        scatter(1, c, gt[rows(c)], dec_v[...], ((1,), (1,)))

    def tpre_total():
        for c in range(C):
            v = total(0, c) + bias[...]
            tps[c] = v
            gather(0, c, 0.5 * v * (1.0 + jnp.tanh(GELU_A * (v + GELU_B * v * v * v))))

    def dtpre(c):
        v = tps[c]
        th = jnp.tanh(GELU_A * (v + GELU_B * v * v * v))
        slope = 0.5 * (1.0 + th) + 0.5 * v * (1.0 - th * th) * GELU_A * (1.0 + 3.0 * GELU_B * v * v)
        gather(1, c, total(1, c) * slope)

    far = carries_gt & (gt_hop >= 3)
    near = jnp.logical_not(far | early_tnorm)
    pl.when(early_tnorm)(tpre_total)
    gt_chunk(0)
    pl.when(far)(tpre_partial)
    gt_chunk(1)

    @pl.when(far)
    def _():
        tpre_total()
        dtpre(0)

    gt_blocks(jnp.clip(gt_done(gt_now), 2 * GN, C * GN), C * GN)

    @pl.when(dx_late)
    def _():
        for c in range(C):
            pass_dx(c)

    pl.when(near)(tpre_partial)
    gt_chunk(2)
    pl.when(near)(tpre_total)
    pl.when(jnp.logical_not(far))(lambda: dtpre(0))
    dtpre(1)
    dtpre(2)
    for c in range(C):
        gathered(0, c)
    for j in range(W // 256):
        js = slice(j * 256, (j + 1) * 256)
        gd_v[:, js] = dot(full[0], gt[:, js], ((0,), (0,)))
    gd_out = local(gd_v, gdec, out_sem.at[0])
    gd_out.start()
    for c in range(C):
        gathered(1, c)
    for j in range(W // 256):
        js = slice(j * 256, (j + 1) * 256)
        ge_v[js, :] = dot(tn[:, js], full[1], ((0,), (0,)))
    ge_out = local(ge_v, genc, out_sem.at[1])
    ge_out.start()
    gbias[...] = jnp.sum(full[1].astype(F32), axis=0, keepdims=True)

    for c in range(C):
        await_bytes(dx.at[rows(c)], go_recv.at[c])
        await_bytes(dx.at[rows(c)], go_send.at[c])
        for s in range(4):
            await_bytes(step_bytes(c, s), rs_send.at[c, s])
        await_bytes(ipb.at[c, pl.ds(0, DP - 1)], ip_send.at[c])
        for kind in range(4):
            await_bytes(rsb.at[0, c, pl.ds(0, DP - 1)], tr_send.at[kind, c])
    await_bytes(sqb.at[pl.ds(0, DP - 1)], sq_sem.at[0])

    @pl.when(p == 0)
    def _():
        await_bytes(tn.at[pl.ds(0, HALF)], tn_send.at[0])
        await_bytes(tn.at[pl.ds(0, HALF)], tn_send.at[1])
        await_bytes(tn, tn_send.at[2])

        await_bytes(sqb.at[pl.ds(0, PIPE - 1)], r0_sem.at[0])

    @pl.when(carries_x0)
    def _():
        @pl.when(z < 7)
        def _():
            await_bytes(tn.at[pl.ds(0, HALF)], tn_send.at[0])

        @pl.when(z > 1)
        def _():
            await_bytes(tn.at[pl.ds(0, HALF)], tn_send.at[1])

        await_bytes(tn, tn_send.at[2])

    @pl.when((p == 1) | (carries_gt & jnp.logical_not(gt_last)))
    def _():
        await_bytes(gt, gt_send.at[0])

    @pl.when((p == 1) | carries_gt)
    def _():
        await_bytes(gt, gt_send.at[1])

    if gt_root_down:
        @pl.when(p == 1)
        def _():
            await_bytes(gt, gt_send.at[2])

    gd_out.wait()
    ge_out.wait()


def body(saved, grads_in, gains, w_in, w_out_t, encoder, enc_bias, decoder, transcoder_norm_gain):
    vmem = pl.BlockSpec(memory_space=pltpu.VMEM)
    anywhere = pl.BlockSpec(memory_space=pl.ANY)
    V = pltpu.VMEM
    DMA = pltpu.SemaphoreType.DMA
    scratch = [
        V((T, W), BF), V((T, W), BF), V((W, H), BF), V((W, H), BF), V((W, L), BF), V((L, W), BF),
        V((2, T, HW), BF), V((C, 2, 3, XR, HW), BF), V((C, 2, XR, HW), F32), V((C, 2, 3, YR, HW), F32),
        V((T, H), BF), V((T, W), F32), V((T, W), BF), V((T, W), BF), V((T, W), BF), V((T, W), BF), V((1, T), F32),
        V((DP, 1, T), F32), V((C, DP, 1, TC), F32), V((T, 128), F32),
        V((2, T, L), BF), V((2, C, DP, TS, L), BF), V((C, TS, L), F32), V((2, T, L), BF),
        V((W, L), F32), V((L, W), F32),
        DMA((8,)), DMA((C, 4)), DMA((C, 4)), DMA((2,)), DMA((C,)), DMA((C,)), DMA((4, C)), DMA((4, C)),
        DMA((2 * NB,)), DMA((3,)), DMA, DMA((C * GN,)), DMA((3,)), DMA((C,)), DMA((C,)), DMA((C,)), DMA((2,)), DMA((2,)),
        pltpu.SemaphoreType.REGULAR,
    ]
    gout, genc, gdec, gbias = pl.pallas_call(
        kernel,
        out_shape=(
            jax.ShapeDtypeStruct((1, T, W), BF),
            jax.ShapeDtypeStruct((W, L), F32),
            jax.ShapeDtypeStruct((L, W), F32),
            jax.ShapeDtypeStruct((1, L), F32),
        ),
        in_specs=[vmem] * 3 + [anywhere] * 6,
        out_specs=(anywhere, anywhere, anywhere, vmem),
        scratch_shapes=scratch,
        compiler_params=pltpu.CompilerParams(
            collective_id=0, has_side_effects=True, vmem_limit_bytes=56 * 1024 * 1024
        ),
        cost_estimate=pl.CostEstimate(flops=5_000_000_000, bytes_accessed=14_000_000, transcendentals=0),
    )(
        gains[0], enc_bias[None], transcoder_norm_gain,
        saved, grads_in, w_in, w_out_t, encoder, decoder,
    )
    return gout, genc, gdec, gbias[0]


def solution(mesh):
    in_specs = (
        P("pipe", None, None, "dp"),
        P("pipe", None, "dp"),
        P("pipe", None, "dp"),
        P("pipe", None, "dp", None),
        P("pipe", None, "dp", None),
        P("dp", "pipe"),
        P("pipe"),
        P("pipe", "dp"),
        P("dp"),
    )
    out_specs = (P("pipe", None, "dp"), P("dp", "pipe"), P("pipe", "dp"), P("pipe"))
    return jax.shard_map(body, mesh=mesh, in_specs=in_specs, out_specs=out_specs, check_vma=False)
```

```python
import functools

import jax
import jax.numpy as jnp
from jax import lax
from jax.experimental import pallas as pl
from jax.experimental.pallas import tpu as pltpu
from jax.sharding import PartitionSpec as P

MESH = pl.DeviceIdType.MESH
BF = jnp.bfloat16
F32 = jnp.float32
MODEL_WIDTH = 16384
T, W, H, L = 768, 1024, 1024, 256
C, TC = 3, 256
HW = H // 2
XR, YR = TC // 4, TC // 16
DP, PIPE = 16, 16
TS = TC // DP
BLK = 32
HALF = T // 2
NB = HALF // BLK
GB = 32
GN = TC // GB
X0_AT = {"00": 8, "10": 10, "01": 14, "20": 16, "11": 18, "02": 20, "21": 22, "12": 24, "22": 64}
GT_LAG = 3
GT_AT = {"13": 3, "0f": 5, "23": 8, "1f": 11, "2f": 14}
GO_AFTER = "00"
Z_UP = 4
GELU_A = 0.7978845608028654
GELU_B = 0.044715


def dot(a, b, dims=((1,), (0,))):
    return lax.dot_general(a, b, (dims, ((), ())), preferred_element_type=F32)


def row_total(block):
    lanes = block[:, 0:128]
    for j in range(1, block.shape[1] // 128):
        lanes = lanes + block[:, j * 128 : (j + 1) * 128]
    return jnp.sum(lanes.T, axis=0, keepdims=True)


def as_columns(row):
    return jnp.broadcast_to(row, (128, row.shape[1])).T


def kernel(
    gains, bias, tgain, saved, gin, win, wout, enc, dec,
    gout, genc, gdec, gbias,
    x_v, gin_v, win_v, wout_v, enc_v, dec_v,
    dhp, p1r, p2s, p2r, dhf, uf, dx, x0, tn, gt, r0,
    sqb, ipb, rcol, part, rsb, tps, full, ge_v, gd_v,
    load_sem, rs_send, rs_recv, sq_sem, ip_send, ip_recv, tr_send, tr_recv,
    tn_recv, tn_send, tnx_recv, gt_recv, gt_send, gtx_recv, go_send, go_recv, out_sem, r0_sem, turn,
):
    p = lax.axis_index("pipe")
    d = lax.axis_index("dp")
    z, core = p // 2, p % 2
    y, x = d // 4, d % 4
    partner = p + 1 - 2 * core
    up, down = (p + 2) % PIPE, (p + PIPE - 2) % PIPE
    first = core == jnp.where(z == 0, 1, 0)
    carries_x0, carries_gt = (core == 1) & (z > 0), (core == 0) & (z > 0)

    def local(src, dst, sem):
        return pltpu.make_async_copy(src, dst, sem)

    def send(src, dst, ssem, rsem, to_p, to_d):
        pltpu.make_async_remote_copy(
            src_ref=src, dst_ref=dst, send_sem=ssem, recv_sem=rsem,
            device_id=(to_p, to_d), device_id_type=MESH,
        ).start()

    def await_bytes(ref, sem):
        pltpu.make_async_copy(ref, ref, sem).wait()

    def rows(c, n=TC):
        return pl.ds(c * n, n)

    gin_l = [local(gin.at[0, rows(c)], gin_v.at[rows(c)], load_sem.at[c]) for c in range(C)]
    wout_l = local(wout.at[0, 0], wout_v, load_sem.at[3])
    x_l = local(saved.at[0, 0], x_v, load_sem.at[4])
    win_l = local(win.at[0, 0], win_v, load_sem.at[5])
    enc_l = local(enc, enc_v, load_sem.at[6])
    dec_l = local(dec, dec_v, load_sem.at[7])
    for copy in (wout_l, *gin_l, x_l, win_l, enc_l, dec_l):
        copy.start()

    barrier = pltpu.get_barrier_semaphore()

    def greet(k, _):
        pl.semaphore_signal(barrier, inc=1, device_id=(p, (d + k) % DP), device_id_type=MESH)
        return 0

    lax.fori_loop(1, DP, greet, 0)
    for by in (1, 2, PIPE - 2, PIPE - 1):
        pl.semaphore_signal(barrier, inc=1, device_id=((p + by) % PIPE, d), device_id_type=MESH)

    @pl.when((p > 2) & (p < PIPE - 2))
    def _():
        pl.semaphore_signal(barrier, inc=1, device_id=(0, d), device_id_type=MESH)

    @pl.when(p == PIPE - 2)
    def _():
        pl.semaphore_signal(barrier, inc=1, device_id=(1, d), device_id_type=MESH)


    place = ((x, y), (y, x))

    def peer(h, axis, k):
        to = (place[h][axis] + k) % 4
        return (y * 4 + to if h == axis else to * 4 + x), to

    def some(start, n):
        return pl.ds(pl.multiple_of(start, n), n)

    def cols(h):
        return slice(h * HW, (h + 1) * HW)

    def dh_partial(c):
        for j in range(H // 256):
            js = slice((j % 2) * 256, (j % 2 + 1) * 256)
            dhp[j // 2, rows(c), js] = dot(gin_v[rows(c)], wout_v[:, j * 256 : (j + 1) * 256]).astype(BF)

    def dh_send():
        def one(c, _):
            for k in (1, 2, 3):
                for h in (0, 1):
                    j, to = peer(h, 0, k)
                    send(dhp.at[h, some(c * TC + to * XR, XR)], p1r.at[c, h, k - 1],
                         rs_send.at[c, 0], rs_recv.at[c, 0], p, j)
            return 0

        lax.fori_loop(0, C, one, 0)

    def step_bytes(c, s):
        return (p1r.at[c], p2r.at[c], p1r.at[c, :, :, pl.ds(0, YR)], p1r.at[c])[s]

    def exchange_step(c, s):
        await_bytes(step_bytes(c, s), rs_recv.at[c, s])
        for h in (0, 1):
            i, j = place[h]
            mine = c * TC + i * XR
            if s == 0:
                v = dhp[h, some(mine, XR)].astype(F32)
                for k in range(3):
                    v = v + p1r[c, h, k].astype(F32)
                p2s[c, h] = v
            elif s == 1:
                v = p2s[c, h, some(j * YR, YR)]
                for k in range(3):
                    v = v + p2r[c, h, k]
                dhf[some(mine + j * YR, YR), cols(h)] = v.astype(BF)
            for k in (1, 2, 3):
                if s == 0:
                    to_d, to = peer(h, 1, k)
                    send(p2s.at[c, h, some(to * YR, YR)], p2r.at[c, h, k - 1],
                         rs_send.at[c, 1], rs_recv.at[c, 1], p, to_d)
                elif s < 3:
                    own = some(mine + j * YR, YR) if s == 1 else some(mine, XR)
                    to_d, _ = peer(h, 1 if s == 1 else 0, k)
                    send(dhf.at[own, cols(h)], dhf.at[own, cols(h)],
                         rs_send.at[c, s + 1], rs_recv.at[c, s + 1], p, to_d)

    def to_group(src_of, dst_of, ssem, rsem):
        def one(k, _):
            j = (d + k) % DP
            send(src_of(j), dst_of(j), ssem, rsem, p, j)
            return 0

        lax.fori_loop(1, DP, one, 0)

    def x0_forward(stream, k):
        blk = pl.ds(pl.multiple_of(stream * HALF + k * BLK, BLK), BLK)
        sem = tn_recv.at[stream * NB + k]
        await_bytes(x0.at[blk], sem)

        @pl.when(z < 6 if stream == 0 else z > 2)
        def _():
            send(x0.at[blk], x0.at[blk], tn_send.at[stream], sem, (up, down)[stream], d)

        send(x0.at[blk], x0.at[blk], tn_send.at[2], tnx_recv, partner, d)

    def x0_done(stream, m):
        late = jnp.where(z == 7, NB, 3 * z - 3) if stream == 0 else jnp.where(z == 1, NB, 21 - 3 * z)
        return jnp.clip(m - late, 0, NB)

    def x0_blocks(lo, hi):
        @pl.when(carries_x0)
        def _():
            for stream in (0, 1):
                def one(k, _, stream=stream):
                    x0_forward(stream, k)
                    return 0

                lax.fori_loop(x0_done(stream, lo), x0_done(stream, hi), one, 0)

    def tnorm():
        @pl.when((p == 1) | carries_gt)
        def _():
            await_bytes(x0, tnx_recv)

        @pl.when(p > 0)
        def _():
            await_bytes(r0, r0_sem.at[1])

        tg = tgain[...].astype(F32)[None, :]
        for c in range(C):
            r = as_columns(r0[:, c * TC : (c + 1) * TC])
            for j in range(W // 128):
                js = slice(j * 128, (j + 1) * 128)
                tn[rows(c), js] = (x0[rows(c), js].astype(F32) * r * tg[:, js]).astype(BF)

    goes_up = z <= Z_UP
    gt_hop = jnp.where(goes_up, z, 8 - z)
    gt_last = (z == Z_UP) | (z == Z_UP + 1)
    gt_next = jnp.where(goes_up, up, down)
    gt_root_down = Z_UP < 7

    def gt_forward(k):
        blk = pl.ds(pl.multiple_of(k * GB, GB), GB)
        await_bytes(gt.at[blk], gt_recv.at[k])

        @pl.when(jnp.logical_not(gt_last))
        def _():
            send(gt.at[blk], gt.at[blk], gt_send.at[0], gt_recv.at[k], gt_next, d)

        send(gt.at[blk], gt.at[blk], gt_send.at[1], gtx_recv.at[k // GN], partner, d)

    def gt_done(m):
        return jnp.clip(m - GT_LAG * (gt_hop - 1), 0, C * GN)

    def gt_blocks(lo, hi):
        def one(k, _):
            gt_forward(k)
            return 0

        @pl.when(carries_gt)
        def _():
            lax.fori_loop(lo, hi, one, 0)

    wout_l.wait()
    for c in range(C):
        gin_l[c].wait()
        dh_partial(c)
    pl.semaphore_wait(barrier, jnp.where(p == 0, DP + PIPE - 2, DP - 1 + 4 + jnp.where(p == 1, 1, 0)))
    pl.when(first)(dh_send)
    x_l.wait()

    @pl.when(p == 0)
    def _():
        x0[...] = x_v[...]

        def one(b, _):
            for way in (0, 1):
                k = lax.rem(b + way * NB, 2 * NB)
                blk = pl.ds(pl.multiple_of(k * BLK, BLK), BLK)
                send(x_v.at[blk], x0.at[blk], tn_send.at[way], tn_recv.at[k], (3, PIPE - 1)[way], d)
            return 0

        lax.fori_loop(0, 2 * NB, one, 0)
        send(x_v, x0, tn_send.at[2], tnx_recv, partner, d)

    for c in range(C):
        xf = x_v[rows(c)].astype(F32)
        sqb[d, :, c * TC : (c + 1) * TC] = row_total(xf * xf)
    to_group(lambda j: sqb.at[d], lambda j: sqb.at[d], sq_sem.at[0], sq_sem.at[1])

    def scale_ready():
        await_bytes(sqb.at[pl.ds(0, DP - 1)], sq_sem.at[1])
        squares = jnp.sum(sqb[...], axis=0)
        scale = lax.rsqrt(squares / MODEL_WIDTH + 1e-05)
        for c in range(C):
            rcol[rows(c)] = as_columns(scale[:, c * TC : (c + 1) * TC])

    @pl.when(p == 0)
    def _():
        scale_ready()
        squares = jnp.sum(sqb[...], axis=0)
        r0[...] = lax.rsqrt(squares / MODEL_WIDTH + 1e-05)

        def one(k, _):
            send(r0, r0, r0_sem.at[0], r0_sem.at[1], k, d)
            return 0

        lax.fori_loop(1, PIPE, one, 0)

    @pl.when(jnp.logical_not(first))
    def _():
        pl.semaphore_wait(turn, 1)
        dh_send()

    win_l.wait()
    enc_l.wait()
    dec_l.wait()

    def back(c):
        lanes = jnp.zeros((1, TC), F32)
        for j in range(W // 256):
            js = slice(j * 256, (j + 1) * 256)
            u = dot(dhf[rows(c)], win_v[js, :], ((1,), (1,))) * gains[:, js].astype(F32)
            uf[rows(c), js] = u
            lanes = lanes + row_total(u * x_v[rows(c), js].astype(F32))
        ipb[c, d] = lanes
        to_group(lambda j: ipb.at[c, d], lambda j: ipb.at[c, d], ip_send.at[c], ip_recv.at[c])

    dx_late = carries_gt & (z > Z_UP + 1)

    def pass_dx(c):
        send(dx.at[rows(c)], gout.at[0, rows(c)], go_send.at[c], go_recv.at[c],
             (p + PIPE - 1) % PIPE, d)

    def finish(c):
        await_bytes(ipb.at[c, pl.ds(0, DP - 1)], ip_recv.at[c])
        inner = as_columns(jnp.sum(ipb[c], axis=0))
        r = rcol[rows(c)]
        coef = r * r * r * inner * (1.0 / MODEL_WIDTH)
        for j in range(W // 128):
            js = slice(j * 128, (j + 1) * 128)
            v = (gin_v[rows(c), js].astype(F32) + r * uf[rows(c), js]
                 - x_v[rows(c), js].astype(F32) * coef).astype(BF)
            dx[rows(c), js] = v

        @pl.when(p == 1)
        def _():
            gt[rows(c)] = dx[rows(c)]

            def one(k, _):
                blk = pl.ds(pl.multiple_of(k * GB, GB), GB)
                send(dx.at[blk], gt.at[blk], gt_send.at[0], gt_recv.at[k], 2, d)
                if gt_root_down:
                    send(dx.at[blk], gt.at[blk], gt_send.at[2], gt_recv.at[k], PIPE - 2, d)
                return 0

            lax.fori_loop(c * GN, (c + 1) * GN, one, 0)
            send(dx.at[rows(c)], gt.at[rows(c)], gt_send.at[1], gtx_recv.at[c], partner, d)

        pl.when(jnp.logical_not(dx_late))(lambda: pass_dx(c))

    def shard(c):
        return pl.ds(pl.multiple_of(c * TC + d * TS, TS), TS)

    def scatter(kind, c, a, b, dims):
        part[kind, rows(c)] = dot(a, b, dims).astype(BF)
        to_group(
            lambda j: part.at[kind, pl.ds(pl.multiple_of(c * TC + j * TS, TS), TS)],
            lambda j: rsb.at[kind, c, d], tr_send.at[2 * kind, c], tr_recv.at[2 * kind, c])
        rsb[kind, c, d] = part[kind, shard(c)]

    def total(kind, c):
        await_bytes(rsb.at[kind, c, pl.ds(0, DP - 1)], tr_recv.at[2 * kind, c])
        return jnp.sum(rsb[kind, c].astype(F32), axis=0)

    def gather(kind, c, values):
        full[kind, shard(c)] = values.astype(BF)
        to_group(
            lambda j: full.at[kind, shard(c)], lambda j: full.at[kind, shard(c)],
            tr_send.at[2 * kind + 1, c], tr_recv.at[2 * kind + 1, c])

    def gathered(kind, c):
        await_bytes(rsb.at[kind, c, pl.ds(0, DP - 1)], tr_recv.at[2 * kind + 1, c])

    def tpre_partial():
        tnorm()
        for c in range(C):
            scatter(0, c, tn[rows(c)], enc_v[...], ((1,), (0,)))

    early_tnorm = carries_x0 | (p == 0)
    order = ("00", "10", "01", "20", "11", "02", "21", "12", "22", "03", "13", "0f", "23", "1f", "2f")
    gt_now = 0
    x0_now = 0
    for step in order:
        c = int(step[0])
        if step in X0_AT:
            x0_blocks(x0_now, X0_AT[step])
            x0_now = X0_AT[step]
        if step[1] == "f":
            finish(c)
        else:
            exchange_step(c, int(step[1]))
            if step[1] == "3":
                back(c)
            if step == GO_AFTER:
                @pl.when(first)
                def _():
                    pl.semaphore_signal(turn, inc=1, device_id=(partner, d), device_id_type=MESH)
        if step == "12":
            pl.when(p > 0)(scale_ready)
        if step == "22":
            pl.when(early_tnorm)(tpre_partial)
        if step in GT_AT:
            gt_blocks(gt_done(gt_now), gt_done(GT_AT[step]))
            gt_now = GT_AT[step]

    def gt_chunk(c):
        if c < C - 1:
            gt_blocks(jnp.clip(gt_done(gt_now), c * GN, (c + 1) * GN), (c + 1) * GN)

        @pl.when(carries_x0 | (p == 0))
        def _():
            await_bytes(gt.at[rows(c)], gtx_recv.at[c])

        scatter(1, c, gt[rows(c)], dec_v[...], ((1,), (1,)))

    def tpre_total():
        for c in range(C):
            v = total(0, c) + bias[...]
            tps[c] = v
            gather(0, c, 0.5 * v * (1.0 + jnp.tanh(GELU_A * (v + GELU_B * v * v * v))))

    def dtpre(c):
        v = tps[c]
        th = jnp.tanh(GELU_A * (v + GELU_B * v * v * v))
        slope = 0.5 * (1.0 + th) + 0.5 * v * (1.0 - th * th) * GELU_A * (1.0 + 3.0 * GELU_B * v * v)
        gather(1, c, total(1, c) * slope)

    far = carries_gt & (gt_hop >= 3)
    near = jnp.logical_not(far | early_tnorm)
    pl.when(early_tnorm)(tpre_total)
    gt_chunk(0)
    pl.when(far)(tpre_partial)
    gt_chunk(1)

    @pl.when(far)
    def _():
        tpre_total()
        dtpre(0)

    gt_blocks(jnp.clip(gt_done(gt_now), 2 * GN, C * GN), C * GN)

    @pl.when(dx_late)
    def _():
        for c in range(C):
            pass_dx(c)

    pl.when(near)(tpre_partial)
    gt_chunk(2)
    pl.when(near)(tpre_total)
    pl.when(jnp.logical_not(far))(lambda: dtpre(0))
    dtpre(1)
    dtpre(2)
    for c in range(C):
        gathered(0, c)
    for j in range(W // 256):
        js = slice(j * 256, (j + 1) * 256)
        gd_v[:, js] = dot(full[0], gt[:, js], ((0,), (0,)))
    gd_out = local(gd_v, gdec, out_sem.at[0])
    gd_out.start()
    for c in range(C):
        gathered(1, c)
    for j in range(W // 256):
        js = slice(j * 256, (j + 1) * 256)
        ge_v[js, :] = dot(tn[:, js], full[1], ((0,), (0,)))
    ge_out = local(ge_v, genc, out_sem.at[1])
    ge_out.start()
    gbias[...] = jnp.sum(full[1].astype(F32), axis=0, keepdims=True)

    for c in range(C):
        await_bytes(dx.at[rows(c)], go_recv.at[c])
        await_bytes(dx.at[rows(c)], go_send.at[c])
        for s in range(4):
            await_bytes(step_bytes(c, s), rs_send.at[c, s])
        await_bytes(ipb.at[c, pl.ds(0, DP - 1)], ip_send.at[c])
        for kind in range(4):
            await_bytes(rsb.at[0, c, pl.ds(0, DP - 1)], tr_send.at[kind, c])
    await_bytes(sqb.at[pl.ds(0, DP - 1)], sq_sem.at[0])

    @pl.when(p == 0)
    def _():
        for way in range(3):
            await_bytes(tn, tn_send.at[way])

        await_bytes(sqb.at[pl.ds(0, PIPE - 1)], r0_sem.at[0])

    @pl.when(carries_x0)
    def _():
        @pl.when(z < 6)
        def _():
            await_bytes(tn.at[pl.ds(0, HALF)], tn_send.at[0])

        @pl.when(z > 2)
        def _():
            await_bytes(tn.at[pl.ds(0, HALF)], tn_send.at[1])

        await_bytes(tn, tn_send.at[2])

    @pl.when((p == 1) | (carries_gt & jnp.logical_not(gt_last)))
    def _():
        await_bytes(gt, gt_send.at[0])

    @pl.when((p == 1) | carries_gt)
    def _():
        await_bytes(gt, gt_send.at[1])

    if gt_root_down:
        @pl.when(p == 1)
        def _():
            await_bytes(gt, gt_send.at[2])

    gd_out.wait()
    ge_out.wait()


PARTS = 2


def hand_over(gout, genc, gdec, gbias, gout_o, genc_o, gdec_o, gbias_o):
    gout_o[...] = gout[...]
    genc_o[...] = genc[...]
    gdec_o[...] = gdec[...]
    gbias_o[...] = gbias[...]


def body(saved, grads_in, gains, w_in, w_out_t, encoder, enc_bias, decoder, transcoder_norm_gain):
    vmem = pl.BlockSpec(memory_space=pltpu.VMEM)
    anywhere = pl.BlockSpec(memory_space=pl.ANY)
    V = pltpu.VMEM
    DMA = pltpu.SemaphoreType.DMA
    scratch = [
        V((T, W), BF), V((T, W), BF), V((W, H), BF), V((W, H), BF), V((W, L), BF), V((L, W), BF),
        V((2, T, HW), BF), V((C, 2, 3, XR, HW), BF), V((C, 2, XR, HW), F32), V((C, 2, 3, YR, HW), F32),
        V((T, H), BF), V((T, W), F32), V((T, W), BF), V((T, W), BF), V((T, W), BF), V((T, W), BF), V((1, T), F32),
        V((DP, 1, T), F32), V((C, DP, 1, TC), F32), V((T, 128), F32),
        V((2, T, L), BF), V((2, C, DP, TS, L), BF), V((C, TS, L), F32), V((2, T, L), BF),
        V((W, L), F32), V((L, W), F32),
        DMA((8,)), DMA((C, 4)), DMA((C, 4)), DMA((2,)), DMA((C,)), DMA((C,)), DMA((4, C)), DMA((4, C)),
        DMA((2 * NB,)), DMA((3,)), DMA, DMA((C * GN,)), DMA((3,)), DMA((C,)), DMA((C,)), DMA((C,)), DMA((2,)), DMA((2,)),
        pltpu.SemaphoreType.REGULAR,
    ]
    gout, genc, gdec, gbias = pl.pallas_call(
        kernel,
        out_shape=(
            jax.ShapeDtypeStruct((1, T, W), BF),
            jax.ShapeDtypeStruct((W, L), F32),
            jax.ShapeDtypeStruct((L, W), F32),
            jax.ShapeDtypeStruct((1, L), F32),
        ),
        in_specs=[vmem] * 3 + [anywhere] * 6,
        out_specs=(anywhere, anywhere, anywhere, vmem),
        scratch_shapes=scratch,
        compiler_params=pltpu.CompilerParams(
            collective_id=0, has_side_effects=True, vmem_limit_bytes=56 * 1024 * 1024
        ),
        cost_estimate=pl.CostEstimate(flops=5_000_000_000, bytes_accessed=14_000_000, transcendentals=0),
    )(
        gains[0], enc_bias[None], transcoder_norm_gain,
        saved, grads_in, w_in, w_out_t, encoder, decoder,
    )
    results = (gout, genc, gdec, gbias)
    blocks = [
        pl.BlockSpec((1, T // PARTS, W), lambda k: (0, k, 0)),
        pl.BlockSpec((W // PARTS, L), lambda k: (k, 0)),
        pl.BlockSpec((L // PARTS, W), lambda k: (k, 0)),
        pl.BlockSpec((1, L), lambda k: (0, 0)),
    ]
    gout, genc, gdec, gbias = pl.pallas_call(
        hand_over,
        grid=(PARTS,),
        out_shape=tuple(jax.ShapeDtypeStruct(a.shape, a.dtype) for a in results),
        in_specs=blocks,
        out_specs=tuple(blocks),
    )(*results)
    return gout, genc, gdec, gbias[0]


def solution(mesh):
    in_specs = (
        P("pipe", None, None, "dp"),
        P("pipe", None, "dp"),
        P("pipe", None, "dp"),
        P("pipe", None, "dp", None),
        P("pipe", None, "dp", None),
        P("dp", "pipe"),
        P("pipe"),
        P("pipe", "dp"),
        P("dp"),
    )
    out_specs = (P("pipe", None, "dp"), P("dp", "pipe"), P("pipe", "dp"), P("pipe"))
    return jax.shard_map(body, mesh=mesh, in_specs=in_specs, out_specs=out_specs, check_vma=False)
```

```python
import functools

import jax
import jax.numpy as jnp
from jax import lax
from jax.experimental import pallas as pl
from jax.experimental.pallas import tpu as pltpu
from jax.sharding import PartitionSpec as P

MESH = pl.DeviceIdType.MESH
BF = jnp.bfloat16
F32 = jnp.float32
MODEL_WIDTH = 16384
T, W, H, L = 768, 1024, 1024, 256
C, TC = 3, 256
HW = H // 2
XR, YR = TC // 4, TC // 16
DP, PIPE = 16, 16
TS = TC // DP
BLK = 32
HALF = T // 2
NB = HALF // BLK
GB = 32
GN = TC // GB
X0_AT = {"00": 8, "10": 10, "01": 14, "20": 16, "11": 18, "02": 20, "21": 22, "12": 24, "22": 64}
GT_LAG = 3
GT_AT = {"13": 3, "0f": 5, "23": 8, "1f": 11, "2f": 14}
GO_AFTER = "00"
Z_UP = 4
GELU_A = 0.7978845608028654
GELU_B = 0.044715


def dot(a, b, dims=((1,), (0,))):
    return lax.dot_general(a, b, (dims, ((), ())), preferred_element_type=F32)


def row_total(block):
    lanes = block[:, 0:128]
    for j in range(1, block.shape[1] // 128):
        lanes = lanes + block[:, j * 128 : (j + 1) * 128]
    return jnp.sum(lanes.T, axis=0, keepdims=True)


def as_columns(row):
    return jnp.broadcast_to(row, (128, row.shape[1])).T


def kernel(
    gains, bias, tgain, saved, gin, win, wout, enc, dec,
    gout, genc, gdec, gbias,
    x_v, gin_v, win_v, wout_v, enc_v, dec_v,
    dhp, p1r, p2s, p2r, dhf, uf, dx, x0, tn, gt, r0,
    sqb, ipb, rcol, part, rsb, tps, full, ge_v, gd_v,
    load_sem, rs_send, rs_recv, sq_sem, ip_send, ip_recv, tr_send, tr_recv,
    tn_recv, tn_send, tnx_recv, gt_recv, gt_send, gtx_recv, go_send, go_recv, out_sem, r0_sem, turn,
):
    p = lax.axis_index("pipe")
    d = lax.axis_index("dp")
    z, core = p // 2, p % 2
    y, x = d // 4, d % 4
    partner = p + 1 - 2 * core
    up, down = (p + 2) % PIPE, (p + PIPE - 2) % PIPE
    first = core == jnp.where(z == 0, 1, 0)
    carries_x0, carries_gt = (core == 1) & (z > 0), (core == 0) & (z > 0)

    def local(src, dst, sem):
        return pltpu.make_async_copy(src, dst, sem)

    def send(src, dst, ssem, rsem, to_p, to_d):
        pltpu.make_async_remote_copy(
            src_ref=src, dst_ref=dst, send_sem=ssem, recv_sem=rsem,
            device_id=(to_p, to_d), device_id_type=MESH,
        ).start()

    def await_bytes(ref, sem):
        pltpu.make_async_copy(ref, ref, sem).wait()

    def rows(c, n=TC):
        return pl.ds(c * n, n)

    gin_l = [local(gin.at[0, rows(c)], gin_v.at[rows(c)], load_sem.at[c]) for c in range(C)]
    wout_l = local(wout.at[0, 0], wout_v, load_sem.at[3])
    x_l = local(saved.at[0, 0], x_v, load_sem.at[4])
    win_l = local(win.at[0, 0], win_v, load_sem.at[5])
    enc_l = local(enc, enc_v, load_sem.at[6])
    dec_l = local(dec, dec_v, load_sem.at[7])
    for copy in (wout_l, *gin_l, x_l, win_l, enc_l, dec_l):
        copy.start()

    barrier = pltpu.get_barrier_semaphore()

    def greet(k, _):
        pl.semaphore_signal(barrier, inc=1, device_id=(p, (d + k) % DP), device_id_type=MESH)
        return 0

    lax.fori_loop(1, DP, greet, 0)
    for by in (1, 2, PIPE - 2, PIPE - 1):
        pl.semaphore_signal(barrier, inc=1, device_id=((p + by) % PIPE, d), device_id_type=MESH)

    @pl.when((p > 2) & (p < PIPE - 2))
    def _():
        pl.semaphore_signal(barrier, inc=1, device_id=(0, d), device_id_type=MESH)

    @pl.when(p == PIPE - 2)
    def _():
        pl.semaphore_signal(barrier, inc=1, device_id=(1, d), device_id_type=MESH)


    place = ((x, y), (y, x))

    def peer(h, axis, k):
        to = (place[h][axis] + k) % 4
        return (y * 4 + to if h == axis else to * 4 + x), to

    def some(start, n):
        return pl.ds(pl.multiple_of(start, n), n)

    def cols(h):
        return slice(h * HW, (h + 1) * HW)

    def dh_partial(c):
        for j in range(H // 256):
            js = slice((j % 2) * 256, (j % 2 + 1) * 256)
            dhp[j // 2, rows(c), js] = dot(gin_v[rows(c)], wout_v[:, j * 256 : (j + 1) * 256]).astype(BF)

    def dh_send():
        def one(c, _):
            for k in (1, 2, 3):
                for h in (0, 1):
                    j, to = peer(h, 0, k)
                    send(dhp.at[h, some(c * TC + to * XR, XR)], p1r.at[c, h, k - 1],
                         rs_send.at[c, 0], rs_recv.at[c, 0], p, j)
            return 0

        lax.fori_loop(0, C, one, 0)

    def step_bytes(c, s):
        return (p1r.at[c], p2r.at[c], p1r.at[c, :, :, pl.ds(0, YR)], p1r.at[c])[s]

    def exchange_step(c, s):
        await_bytes(step_bytes(c, s), rs_recv.at[c, s])
        for h in (0, 1):
            i, j = place[h]
            mine = c * TC + i * XR
            if s == 0:
                v = dhp[h, some(mine, XR)].astype(F32)
                for k in range(3):
                    v = v + p1r[c, h, k].astype(F32)
                p2s[c, h] = v.astype(BF)
            elif s == 1:
                v = p2s[c, h, some(j * YR, YR)].astype(F32)
                for k in range(3):
                    v = v + p2r[c, h, k].astype(F32)
                dhf[some(mine + j * YR, YR), cols(h)] = v.astype(BF)
            for k in (1, 2, 3):
                if s == 0:
                    to_d, to = peer(h, 1, k)
                    send(p2s.at[c, h, some(to * YR, YR)], p2r.at[c, h, k - 1],
                         rs_send.at[c, 1], rs_recv.at[c, 1], p, to_d)
                elif s < 3:
                    own = some(mine + j * YR, YR) if s == 1 else some(mine, XR)
                    to_d, _ = peer(h, 1 if s == 1 else 0, k)
                    send(dhf.at[own, cols(h)], dhf.at[own, cols(h)],
                         rs_send.at[c, s + 1], rs_recv.at[c, s + 1], p, to_d)

    def to_group(src_of, dst_of, ssem, rsem):
        def one(k, _):
            j = (d + k) % DP
            send(src_of(j), dst_of(j), ssem, rsem, p, j)
            return 0

        lax.fori_loop(1, DP, one, 0)

    def x0_forward(stream, k):
        blk = pl.ds(pl.multiple_of(stream * HALF + k * BLK, BLK), BLK)
        sem = tn_recv.at[stream * NB + k]
        await_bytes(x0.at[blk], sem)

        @pl.when(z < 6 if stream == 0 else z > 2)
        def _():
            send(x0.at[blk], x0.at[blk], tn_send.at[stream], sem, (up, down)[stream], d)

        send(x0.at[blk], x0.at[blk], tn_send.at[2], tnx_recv, partner, d)

    def x0_done(stream, m):
        late = jnp.where(z == 7, NB, 3 * z - 3) if stream == 0 else jnp.where(z == 1, NB, 21 - 3 * z)
        return jnp.clip(m - late, 0, NB)

    def x0_blocks(lo, hi):
        @pl.when(carries_x0)
        def _():
            for stream in (0, 1):
                def one(k, _, stream=stream):
                    x0_forward(stream, k)
                    return 0

                lax.fori_loop(x0_done(stream, lo), x0_done(stream, hi), one, 0)

    def tnorm():
        @pl.when((p == 1) | carries_gt)
        def _():
            await_bytes(x0, tnx_recv)

        @pl.when(p > 0)
        def _():
            await_bytes(r0, r0_sem.at[1])

        tg = tgain[...].astype(F32)[None, :]
        for c in range(C):
            r = as_columns(r0[:, c * TC : (c + 1) * TC])
            for j in range(W // 128):
                js = slice(j * 128, (j + 1) * 128)
                tn[rows(c), js] = (x0[rows(c), js].astype(F32) * r * tg[:, js]).astype(BF)

    goes_up = z <= Z_UP
    gt_hop = jnp.where(goes_up, z, 8 - z)
    gt_last = (z == Z_UP) | (z == Z_UP + 1)
    gt_next = jnp.where(goes_up, up, down)
    gt_root_down = Z_UP < 7

    def gt_forward(k):
        blk = pl.ds(pl.multiple_of(k * GB, GB), GB)
        await_bytes(gt.at[blk], gt_recv.at[k])

        @pl.when(jnp.logical_not(gt_last))
        def _():
            send(gt.at[blk], gt.at[blk], gt_send.at[0], gt_recv.at[k], gt_next, d)

        send(gt.at[blk], gt.at[blk], gt_send.at[1], gtx_recv.at[k // GN], partner, d)

    def gt_done(m):
        return jnp.clip(m - GT_LAG * (gt_hop - 1), 0, C * GN)

    def gt_blocks(lo, hi):
        def one(k, _):
            gt_forward(k)
            return 0

        @pl.when(carries_gt)
        def _():
            lax.fori_loop(lo, hi, one, 0)

    wout_l.wait()
    for c in range(C):
        gin_l[c].wait()
        dh_partial(c)
    pl.semaphore_wait(barrier, jnp.where(p == 0, DP + PIPE - 2, DP - 1 + 4 + jnp.where(p == 1, 1, 0)))
    pl.when(first)(dh_send)
    x_l.wait()

    @pl.when(p == 0)
    def _():
        x0[...] = x_v[...]

        def one(b, _):
            for way in (0, 1):
                k = lax.rem(b + way * NB, 2 * NB)
                blk = pl.ds(pl.multiple_of(k * BLK, BLK), BLK)
                send(x_v.at[blk], x0.at[blk], tn_send.at[way], tn_recv.at[k], (3, PIPE - 1)[way], d)
            return 0

        lax.fori_loop(0, 2 * NB, one, 0)
        send(x_v, x0, tn_send.at[2], tnx_recv, partner, d)

    for c in range(C):
        xf = x_v[rows(c)].astype(F32)
        sqb[d, :, c * TC : (c + 1) * TC] = row_total(xf * xf)
    to_group(lambda j: sqb.at[d], lambda j: sqb.at[d], sq_sem.at[0], sq_sem.at[1])

    def scale_ready():
        await_bytes(sqb.at[pl.ds(0, DP - 1)], sq_sem.at[1])
        squares = jnp.sum(sqb[...], axis=0)
        scale = lax.rsqrt(squares / MODEL_WIDTH + 1e-05)
        for c in range(C):
            rcol[rows(c)] = as_columns(scale[:, c * TC : (c + 1) * TC])

    @pl.when(p == 0)
    def _():
        scale_ready()
        squares = jnp.sum(sqb[...], axis=0)
        r0[...] = lax.rsqrt(squares / MODEL_WIDTH + 1e-05)

        def one(k, _):
            send(r0, r0, r0_sem.at[0], r0_sem.at[1], k, d)
            return 0

        lax.fori_loop(1, PIPE, one, 0)

    @pl.when(jnp.logical_not(first))
    def _():
        pl.semaphore_wait(turn, 1)
        dh_send()

    win_l.wait()
    enc_l.wait()
    dec_l.wait()

    def back(c):
        lanes = jnp.zeros((1, TC), F32)
        for j in range(W // 256):
            js = slice(j * 256, (j + 1) * 256)
            u = dot(dhf[rows(c)], win_v[js, :], ((1,), (1,))) * gains[:, js].astype(F32)
            uf[rows(c), js] = u
            lanes = lanes + row_total(u * x_v[rows(c), js].astype(F32))
        ipb[c, d] = lanes
        to_group(lambda j: ipb.at[c, d], lambda j: ipb.at[c, d], ip_send.at[c], ip_recv.at[c])

    dx_late = carries_gt & (z > Z_UP + 1)

    def pass_dx(c):
        send(dx.at[rows(c)], gout.at[0, rows(c)], go_send.at[c], go_recv.at[c],
             (p + PIPE - 1) % PIPE, d)

    def finish(c):
        await_bytes(ipb.at[c, pl.ds(0, DP - 1)], ip_recv.at[c])
        inner = as_columns(jnp.sum(ipb[c], axis=0))
        r = rcol[rows(c)]
        coef = r * r * r * inner * (1.0 / MODEL_WIDTH)
        for j in range(W // 128):
            js = slice(j * 128, (j + 1) * 128)
            v = (gin_v[rows(c), js].astype(F32) + r * uf[rows(c), js]
                 - x_v[rows(c), js].astype(F32) * coef).astype(BF)
            dx[rows(c), js] = v

        @pl.when(p == 1)
        def _():
            gt[rows(c)] = dx[rows(c)]

            def one(k, _):
                blk = pl.ds(pl.multiple_of(k * GB, GB), GB)
                send(dx.at[blk], gt.at[blk], gt_send.at[0], gt_recv.at[k], 2, d)
                if gt_root_down:
                    send(dx.at[blk], gt.at[blk], gt_send.at[2], gt_recv.at[k], PIPE - 2, d)
                return 0

            lax.fori_loop(c * GN, (c + 1) * GN, one, 0)
            send(dx.at[rows(c)], gt.at[rows(c)], gt_send.at[1], gtx_recv.at[c], partner, d)

        pl.when(jnp.logical_not(dx_late))(lambda: pass_dx(c))

    def shard(c):
        return pl.ds(pl.multiple_of(c * TC + d * TS, TS), TS)

    def scatter(kind, c, a, b, dims):
        part[kind, rows(c)] = dot(a, b, dims).astype(BF)
        to_group(
            lambda j: part.at[kind, pl.ds(pl.multiple_of(c * TC + j * TS, TS), TS)],
            lambda j: rsb.at[kind, c, d], tr_send.at[2 * kind, c], tr_recv.at[2 * kind, c])
        rsb[kind, c, d] = part[kind, shard(c)]

    def total(kind, c):
        await_bytes(rsb.at[kind, c, pl.ds(0, DP - 1)], tr_recv.at[2 * kind, c])
        return jnp.sum(rsb[kind, c].astype(F32), axis=0)

    def gather(kind, c, values):
        full[kind, shard(c)] = values.astype(BF)
        to_group(
            lambda j: full.at[kind, shard(c)], lambda j: full.at[kind, shard(c)],
            tr_send.at[2 * kind + 1, c], tr_recv.at[2 * kind + 1, c])

    def gathered(kind, c):
        await_bytes(rsb.at[kind, c, pl.ds(0, DP - 1)], tr_recv.at[2 * kind + 1, c])

    def tpre_partial():
        tnorm()
        for c in range(C):
            scatter(0, c, tn[rows(c)], enc_v[...], ((1,), (0,)))

    early_tnorm = carries_x0 | (p == 0)
    order = ("00", "10", "01", "20", "11", "02", "21", "12", "22", "03", "13", "0f", "23", "1f", "2f")
    gt_now = 0
    x0_now = 0
    for step in order:
        c = int(step[0])
        if step in X0_AT:
            x0_blocks(x0_now, X0_AT[step])
            x0_now = X0_AT[step]
        if step[1] == "f":
            finish(c)
        else:
            exchange_step(c, int(step[1]))
            if step[1] == "3":
                back(c)
            if step == GO_AFTER:
                @pl.when(first)
                def _():
                    pl.semaphore_signal(turn, inc=1, device_id=(partner, d), device_id_type=MESH)
        if step == "12":
            pl.when(p > 0)(scale_ready)
        if step == "22":
            pl.when(early_tnorm)(tpre_partial)
        if step in GT_AT:
            gt_blocks(gt_done(gt_now), gt_done(GT_AT[step]))
            gt_now = GT_AT[step]

    def gt_chunk(c):
        if c < C - 1:
            gt_blocks(jnp.clip(gt_done(gt_now), c * GN, (c + 1) * GN), (c + 1) * GN)

        @pl.when(carries_x0 | (p == 0))
        def _():
            await_bytes(gt.at[rows(c)], gtx_recv.at[c])

        scatter(1, c, gt[rows(c)], dec_v[...], ((1,), (1,)))

    def tpre_total():
        for c in range(C):
            v = total(0, c) + bias[...]
            tps[c] = v
            gather(0, c, 0.5 * v * (1.0 + jnp.tanh(GELU_A * (v + GELU_B * v * v * v))))

    def dtpre(c):
        v = tps[c]
        th = jnp.tanh(GELU_A * (v + GELU_B * v * v * v))
        slope = 0.5 * (1.0 + th) + 0.5 * v * (1.0 - th * th) * GELU_A * (1.0 + 3.0 * GELU_B * v * v)
        gather(1, c, total(1, c) * slope)

    far = carries_gt & (gt_hop >= 3)
    near = jnp.logical_not(far | early_tnorm)
    pl.when(early_tnorm)(tpre_total)
    gt_chunk(0)
    pl.when(far)(tpre_partial)
    gt_chunk(1)

    @pl.when(far)
    def _():
        tpre_total()
        dtpre(0)

    gt_blocks(jnp.clip(gt_done(gt_now), 2 * GN, C * GN), C * GN)

    @pl.when(dx_late)
    def _():
        for c in range(C):
            pass_dx(c)

    pl.when(near)(tpre_partial)
    gt_chunk(2)
    pl.when(near)(tpre_total)
    pl.when(jnp.logical_not(far))(lambda: dtpre(0))
    dtpre(1)
    dtpre(2)
    for c in range(C):
        gathered(0, c)
    for j in range(W // 256):
        js = slice(j * 256, (j + 1) * 256)
        gd_v[:, js] = dot(full[0], gt[:, js], ((0,), (0,)))
    gd_out = local(gd_v, gdec, out_sem.at[0])
    gd_out.start()
    for part_of, waits in ((slice(0, 2 * TC), (0, 1)), (slice(2 * TC, T), (2,))):
        for c in waits:
            gathered(1, c)
        for j in range(W // 256):
            js = slice(j * 256, (j + 1) * 256)
            more = dot(tn[part_of, js], full[1, part_of], ((0,), (0,)))
            ge_v[js, :] = more if waits[0] == 0 else ge_v[js, :] + more
    ge_out = local(ge_v, genc, out_sem.at[1])
    ge_out.start()
    gbias[...] = jnp.sum(full[1].astype(F32), axis=0, keepdims=True)

    for c in range(C):
        await_bytes(dx.at[rows(c)], go_recv.at[c])
        await_bytes(dx.at[rows(c)], go_send.at[c])
        for s in range(4):
            await_bytes(step_bytes(c, s), rs_send.at[c, s])
        await_bytes(ipb.at[c, pl.ds(0, DP - 1)], ip_send.at[c])
        for kind in range(4):
            await_bytes(rsb.at[0, c, pl.ds(0, DP - 1)], tr_send.at[kind, c])
    await_bytes(sqb.at[pl.ds(0, DP - 1)], sq_sem.at[0])

    @pl.when(p == 0)
    def _():
        for way in range(3):
            await_bytes(tn, tn_send.at[way])

        await_bytes(sqb.at[pl.ds(0, PIPE - 1)], r0_sem.at[0])

    @pl.when(carries_x0)
    def _():
        @pl.when(z < 6)
        def _():
            await_bytes(tn.at[pl.ds(0, HALF)], tn_send.at[0])

        @pl.when(z > 2)
        def _():
            await_bytes(tn.at[pl.ds(0, HALF)], tn_send.at[1])

        await_bytes(tn, tn_send.at[2])

    @pl.when((p == 1) | (carries_gt & jnp.logical_not(gt_last)))
    def _():
        await_bytes(gt, gt_send.at[0])

    @pl.when((p == 1) | carries_gt)
    def _():
        await_bytes(gt, gt_send.at[1])

    if gt_root_down:
        @pl.when(p == 1)
        def _():
            await_bytes(gt, gt_send.at[2])

    gd_out.wait()
    ge_out.wait()


PARTS = 2


def hand_over(gout, genc, gdec, gbias, gout_o, genc_o, gdec_o, gbias_o):
    gout_o[...] = gout[...]
    genc_o[...] = genc[...]
    gdec_o[...] = gdec[...]
    gbias_o[...] = gbias[...]


def body(saved, grads_in, gains, w_in, w_out_t, encoder, enc_bias, decoder, transcoder_norm_gain):
    vmem = pl.BlockSpec(memory_space=pltpu.VMEM)
    anywhere = pl.BlockSpec(memory_space=pl.ANY)
    V = pltpu.VMEM
    DMA = pltpu.SemaphoreType.DMA
    scratch = [
        V((T, W), BF), V((T, W), BF), V((W, H), BF), V((W, H), BF), V((W, L), BF), V((L, W), BF),
        V((2, T, HW), BF), V((C, 2, 3, XR, HW), BF), V((C, 2, XR, HW), BF), V((C, 2, 3, YR, HW), BF),
        V((T, H), BF), V((T, W), F32), V((T, W), BF), V((T, W), BF), V((T, W), BF), V((T, W), BF), V((1, T), F32),
        V((DP, 1, T), F32), V((C, DP, 1, TC), F32), V((T, 128), F32),
        V((2, T, L), BF), V((2, C, DP, TS, L), BF), V((C, TS, L), F32), V((2, T, L), BF),
        V((W, L), F32), V((L, W), F32),
        DMA((8,)), DMA((C, 4)), DMA((C, 4)), DMA((2,)), DMA((C,)), DMA((C,)), DMA((4, C)), DMA((4, C)),
        DMA((2 * NB,)), DMA((3,)), DMA, DMA((C * GN,)), DMA((3,)), DMA((C,)), DMA((C,)), DMA((C,)), DMA((2,)), DMA((2,)),
        pltpu.SemaphoreType.REGULAR,
    ]
    gout, genc, gdec, gbias = pl.pallas_call(
        kernel,
        out_shape=(
            jax.ShapeDtypeStruct((1, T, W), BF),
            jax.ShapeDtypeStruct((W, L), F32),
            jax.ShapeDtypeStruct((L, W), F32),
            jax.ShapeDtypeStruct((1, L), F32),
        ),
        in_specs=[vmem] * 3 + [anywhere] * 6,
        out_specs=(anywhere, anywhere, anywhere, vmem),
        scratch_shapes=scratch,
        compiler_params=pltpu.CompilerParams(
            collective_id=0, has_side_effects=True, vmem_limit_bytes=56 * 1024 * 1024
        ),
        cost_estimate=pl.CostEstimate(flops=5_000_000_000, bytes_accessed=14_000_000, transcendentals=0),
    )(
        gains[0], enc_bias[None], transcoder_norm_gain,
        saved, grads_in, w_in, w_out_t, encoder, decoder,
    )
    results = (gout, genc, gdec, gbias)
    blocks = [
        pl.BlockSpec((1, T // PARTS, W), lambda k: (0, k, 0)),
        pl.BlockSpec((W // PARTS, L), lambda k: (k, 0)),
        pl.BlockSpec((L // PARTS, W), lambda k: (k, 0)),
        pl.BlockSpec((1, L), lambda k: (0, 0)),
    ]
    gout, genc, gdec, gbias = pl.pallas_call(
        hand_over,
        grid=(PARTS,),
        out_shape=tuple(jax.ShapeDtypeStruct(a.shape, a.dtype) for a in results),
        in_specs=blocks,
        out_specs=tuple(blocks),
    )(*results)
    return gout, genc, gdec, gbias[0]


def solution(mesh):
    in_specs = (
        P("pipe", None, None, "dp"),
        P("pipe", None, "dp"),
        P("pipe", None, "dp"),
        P("pipe", None, "dp", None),
        P("pipe", None, "dp", None),
        P("dp", "pipe"),
        P("pipe"),
        P("pipe", "dp"),
        P("dp"),
    )
    out_specs = (P("pipe", None, "dp"), P("dp", "pipe"), P("pipe", "dp"), P("pipe"))
    return jax.shard_map(body, mesh=mesh, in_specs=in_specs, out_specs=out_specs, check_vma=False)
```
